32 devices in a mesh: gx: 4 (over z), gy: 8 (over y, x, core).
Axes of the slice: x: 2, y: 2, z: 4, core: 2. Of those that a mesh axis runs over, the one named last changes fastest.
Arguments:
- initial_guess: float32 [5, 32, 256, 128], P(None, 'gx', 'gy'), may hold values from -6 to 6
- right_side: float32 [5, 32, 256, 128], P(None, 'gx', 'gy'), may hold values from -6 to 6
- coefficients: float32 [5, 32, 256, 128], P(None, 'gx', 'gy'), may hold values from 0.3 to 3
- tunnel_mask: int32 [32, 256, 128], P('gx', 'gy'), may hold values 0 or 1
- stencil: float32 [27, 5, 5], replicated, may hold values from -0.03 to 1.15, as said below
Outputs:
- fine_iterate: float32 [5, 32, 256, 128], P(None, 'gx', 'gy')
- middle_iterate: float32 [5, 16, 128, 128], P(None, 'gx', 'gy')
- lower_iterate: float32 [5, 8, 64, 128], P(None, 'gx', 'gy')
- coarse_residual: float32 [5, 4, 32, 128], P(None, 'gx', 'gy')
The draws below stay inside these ranges and needn't reach their ends.
Inputs may be any that keep to these rules, and one draw needn't show every extreme that they name: `stencil`: entries of all 27 blocks; the centre block's diagonal lies in 0.85 to 1.15; off-centre blocks have diagonal entries in -0.025 to -0.01 and off-diagonal entries in -0.004 to 0.004; the centre block's off-diagonal entries lie in -0.02 to 0.02.
All inputs are finite; a program needn't handle non-finite values. No bound on the sum of `tunnel_mask` on one device may be relied on, other than what follows from the above.
Results may differ from the reference program's by a relative error of at most 0.00029.
Values sent between devices are 32-bit elements; how exact they have to be, the bound alone decides.
A program may use at most 64 MiB of HBM per device.

```python
import math
import jax
import jax.numpy as jnp
from jax import lax

COMP = 5
SWEEPS = 2
CZ = 128
NX = 32
NY = 256


def draw_stencil(key, part):
    key_off, key_link, key_centre, key_cross = jax.random.split(key, 4)
    identity = jnp.eye(COMP, dtype=jnp.float32)
    scatter_part = jax.random.uniform(key_off, (27, COMP, COMP), jnp.float32, -0.004, 0.004)
    link = -jax.random.uniform(key_link, (27, COMP), jnp.float32, 0.01, 0.025)
    blocks = scatter_part * (1.0 - identity) + link[:, :, None] * identity
    centre = jax.random.uniform(key_centre, (COMP,), jnp.float32, 0.85, 1.15)
    cross = jax.random.uniform(key_cross, (COMP, COMP), jnp.float32, -0.02, 0.02)
    centre_block = cross * (1.0 - identity) + centre[:, None] * identity
    return blocks.at[13].set(centre_block)


def set_ends(array, rng, smallest, largest):
    extent = array.shape
    index_at = [jax.random.randint(jax.random.fold_in(rng, axis), (), 0, extent[axis]) for axis in range(len(extent))]
    array = array.at[tuple(index_at)].set(smallest)
    longest = extent.index(max(extent))
    index_at[longest] = (index_at[longest] + 1) % extent[longest]
    return array.at[tuple(index_at)].set(largest)


def block_scale(key, extent, cuts, smallest, top_value):
    def one(axis_at, parts):
        draws = jax.random.uniform(jax.random.fold_in(jax.random.fold_in(key, 6), axis_at), (parts,), jnp.float32, smallest / len(cuts), top_value / len(cuts))
        return jnp.repeat(jnp.exp(draws), extent[axis_at] // parts).reshape((-1,) + (1,) * (len(extent) - axis_at - 1))

    gain = one(*cuts[0])
    for cut in cuts[1:]:
        gain = gain * one(*cut)
    return gain


def noise(key, extent, deviation, limit, cuts=(), kind=jnp.bfloat16):
    array = deviation * jax.random.normal(key, extent, jnp.float32)
    if cuts:
        array = array * block_scale(key, extent, cuts, -0.22, 0.18)
    return jnp.clip(array, -limit, limit).astype(kind)


def setup_inputs(seed: int = 0) -> dict:
    key_list = jax.random.split(jax.random.key(seed), 6)
    initial_guess = noise(key_list[0], (COMP, NX, NY, CZ), 1.0, 6.0, ((1, 4), (2, 8)), jnp.float32)
    right_side = noise(key_list[1], (COMP, NX, NY, CZ), 1.0, 6.0, ((1, 4), (2, 8)), jnp.float32)
    coefficients = jnp.clip(jnp.exp(math.log(3.0) - 2.3025851 * jax.random.uniform(key_list[2], (COMP, NX, NY, CZ), jnp.float32) ** block_scale(key_list[2], (COMP, NX, NY, CZ), ((1, 4), (2, 8)), -0.2, 0.2)), 0.3, 3.0)
    tunnel_mask = set_ends((jax.random.randint(key_list[3], (NX, NY, CZ), 0, 8) < 7).astype(jnp.int32), jax.random.fold_in(key_list[3], 1), 0, 1)
    stencil = draw_stencil(jax.random.fold_in(key_list[5], 71), 0)
    return dict(initial_guess=initial_guess, right_side=right_side, coefficients=coefficients, tunnel_mask=tunnel_mask, stencil=stencil)


DAMPING = 0.7
WEIGHTS = (0.125, 0.375, 0.375, 0.125)


def pad_plane(values):
    return jnp.pad(values, ((0, 0), (1, 1), (1, 1), (0, 0)))


def operate(iterate, conduct, rock_share, stencil, faces):
    masked = rock_share[None] * iterate
    padded = jnp.pad(faces(masked), ((0, 0), (0, 0), (0, 0), (1, 1)))
    extent_x, extent_y, extent_z = iterate.shape[1], iterate.shape[2], iterate.shape[3]
    summed = jnp.zeros(iterate.shape, jnp.float32)
    for offset in range(27):
        shift_x, shift_y, shift_z = offset // 9, (offset // 3) % 3, offset % 3
        shifted = padded[:, shift_x:shift_x + extent_x, shift_y:shift_y + extent_y, shift_z:shift_z + extent_z]
        summed = summed + jnp.einsum("ab,bxyz->axyz", stencil[offset], shifted, precision=lax.Precision.HIGHEST)
    return conduct * rock_share[None] * summed


def smooth_level(iterate, forcing, conduct, rock_share, stencil, faces):
    diagonal = conduct * jnp.diagonal(stencil[13])[:, None, None, None]
    source = rock_share[None] * forcing
    if iterate is None:
        iterate = DAMPING * source / diagonal
        remaining = SWEEPS - 1
    else:
        remaining = SWEEPS
    for sweep_index in range(remaining):
        iterate = iterate + DAMPING * (source - operate(iterate, conduct, rock_share, stencil, faces)) / diagonal
    residual = source - operate(iterate, conduct, rock_share, stencil, faces)
    return iterate, residual


def shrink(padded):
    extent_x = padded.shape[1] - 2
    along_x = sum(WEIGHTS[weight_index] * padded[:, weight_index:weight_index + extent_x - 1:2] for weight_index in range(4))
    extent_y = padded.shape[2] - 2
    return sum(WEIGHTS[weight_index] * along_x[:, :, weight_index:weight_index + extent_y - 1:2] for weight_index in range(4))


def coarsen(values):
    leading = values.shape[:-3]
    extent_x, extent_y, extent_z = values.shape[-3], values.shape[-2], values.shape[-1]
    reshaped = values.reshape(leading + (extent_x // 2, 2, extent_y // 2, 2, extent_z))
    return reshaped.mean(axis=(-4, -2))


def reference(initial_guess, right_side, coefficients, tunnel_mask, stencil):
    rock_share = tunnel_mask.astype(jnp.float32)
    conduct = coefficients
    fine_iterate, residual = smooth_level(initial_guess, right_side, conduct, rock_share, stencil, pad_plane)
    kept = [fine_iterate]
    for layer_index in range(2):
        forcing = shrink(pad_plane(residual))
        conduct = coarsen(conduct)
        rock_share = coarsen(rock_share)
        iterate, residual = smooth_level(None, forcing, conduct, rock_share, stencil, pad_plane)
        kept.append(iterate)
    forcing = shrink(pad_plane(residual))
    conduct = coarsen(conduct)
    rock_share = coarsen(rock_share)
    iterate, coarse_residual = smooth_level(None, forcing, conduct, rock_share, stencil, pad_plane)
    return kept[0], kept[1], kept[2], coarse_residual
```

```python
import functools

import jax
import jax.numpy as jnp
import numpy as np
from jax import lax
from jax.experimental import pallas as pl
from jax.experimental.pallas import tpu as pltpu
from jax.sharding import PartitionSpec as P

MESH = pl.DeviceIdType.MESH
COMP = 5
DAMPING = 0.7
WEIGHTS = (0.125, 0.375, 0.375, 0.125)
LEVELS = 4
ROUNDS = (4, 3, 3, 2)
DIRECTIONS = [(dx, dy) for dx in (-1, 0, 1) for dy in (-1, 0, 1) if (dx, dy) != (0, 0)]
FACES_Y = [i for i, d in enumerate(DIRECTIONS) if d[0] == 0]
FACES_X = [i for i, d in enumerate(DIRECTIONS) if d[0] != 0]
F32, BF16 = jnp.float32, jnp.bfloat16


class Level:
    def __init__(self, extent_x, extent_y):
        self.x, self.y = extent_x, extent_y
        self.yp = max(8, extent_y)
        self.rows = -(-COMP * self.yp // 16) * 16
        self.depth = self.rows + 16
        self.pairs = max(1, extent_x // 2)
        self.wide = min(2, extent_x)
        pos = np.full((self.depth,), -100, np.int32)
        unknown = np.zeros((self.depth,), np.int32)
        for b in range(COMP):
            pos[b * self.yp : b * self.yp + self.y] = np.arange(self.y)
            unknown[b * self.yp : (b + 1) * self.yp] = b
            pos[self.rows + b], unknown[self.rows + b] = -1, b
            pos[self.rows + 8 + b], unknown[self.rows + 8 + b] = self.y, b
        self.pos = np.tile(pos, 9)[None]
        hot = np.zeros((15, 3 * self.depth), np.float32)
        for ox in range(3):
            hot[ox * COMP + unknown, ox * self.depth + np.arange(self.depth)] = 1.0
        self.hot = np.tile(hot, (1, 3))


def transfer_matrices(fine, coarse):
    restrict = np.zeros((coarse.rows, fine.depth), np.float32)
    mean = np.zeros((coarse.rows, fine.rows), np.float32)
    for a in range(COMP):
        for j in range(coarse.y):
            row = a * coarse.yp + j
            for t in range(4):
                y = 2 * j - 1 + t
                if y < 0:
                    column = fine.rows + a
                elif y >= fine.y:
                    column = fine.rows + 8 + a
                else:
                    column = a * fine.yp + y
                restrict[row, column] = WEIGHTS[t]
            mean[row, a * fine.yp + 2 * j] = 0.5
            mean[row, a * fine.yp + 2 * j + 1] = 0.5
    return np.tile(restrict, (1, 2)), np.tile(mean, (1, 2))


def split(values):
    high = values.astype(BF16)
    return high, (values - high.astype(F32)).astype(BF16)


def kernel(levels, count_x, count_y, *refs):
    refs = list(refs)
    take = lambda n: [refs.pop(0) for _ in range(n)]
    guess_ref, right_ref, conduct_ref, mask_ref, diag_ref = take(5)
    spread = take(LEVELS)
    place = take(LEVELS)
    restrict_m = take(LEVELS - 1)
    mean_m = take(LEVELS - 1)
    outs = take(4)
    weight = take(LEVELS)
    high, low = take(LEVELS), take(LEVELS)
    conduct, share, force, ratio, gain, state = [take(LEVELS) for _ in range(6)]
    edge, side, side_out = [take(sum(ROUNDS)) for _ in range(3)]
    send_sem, recv_sem = take(2)

    at_x, at_y = lax.axis_index("gx"), lax.axis_index("gy")

    def inside(dx, dy):
        okay = None
        for shift, at, count in ((dx, at_x, count_x), (dy, at_y, count_y)):
            if shift:
                here = at > 0 if shift < 0 else at < count - 1
                okay = here if okay is None else jnp.logical_and(okay, here)
        return okay

    first_round = [sum(ROUNDS[:l]) for l in range(LEVELS)]

    for l, lev in enumerate(levels):
        for rnd in range(first_round[l], first_round[l] + ROUNDS[l]):
            edge[rnd][0] = jnp.zeros((lev.rows, 128), F32)
            edge[rnd][lev.x + 1] = jnp.zeros((lev.rows, 128), F32)
            side[rnd][...] = jnp.zeros(side[rnd].shape, F32)
            side_out[rnd][...] = jnp.zeros(side_out[rnd].shape, F32)

    barrier = pltpu.get_barrier_semaphore()
    for dx, dy in DIRECTIONS:
        @pl.when(inside(dx, dy))
        def _(dx=dx, dy=dy):
            pl.semaphore_signal(barrier, inc=1, device_id=(at_x + dx, at_y + dy), device_id_type=MESH)

    span = lambda at, count: 3 - jnp.where(at == 0, 1, 0) - jnp.where(at == count - 1, 1, 0)
    neighbours = span(at_x, count_x) * span(at_y, count_y) - 1

    def copy(l, rnd, index):
        lev = levels[l]
        dx, dy = DIRECTIONS[index]
        mine = lev.x if dx > 0 else 1
        theirs = 0 if dx > 0 else lev.x + 1
        if dy == 0:
            src, dst = edge[rnd].at[mine], edge[rnd].at[theirs]
        else:
            out_at, in_at = (1, 0) if dy > 0 else (0, 1)
            if dx == 0:
                src = side_out[rnd].at[out_at]
                dst = side[rnd].at[in_at, pl.ds(1, lev.x)]
            else:
                src = side_out[rnd].at[out_at, mine - 1]
                dst = side[rnd].at[in_at, theirs]
        return pltpu.make_async_remote_copy(
            src_ref=src,
            dst_ref=dst,
            send_sem=send_sem.at[rnd, index],
            recv_sem=recv_sem.at[rnd, index],
            device_id=(at_x + dx, at_y + dy),
            device_id_type=MESH,
        )

    def send(l, rnd):
        for index in FACES_X + FACES_Y:
            @pl.when(inside(*DIRECTIONS[index]))
            def _(index=index):
                copy(l, rnd, index).start()

    def receive(l, rnd, which):
        for index in which:
            dx, dy = DIRECTIONS[index]
            @pl.when(inside(-dx, -dy))
            def _(index=index):
                copy(l, rnd, index).wait_recv()

    def finish(l, rnd):
        for index in range(len(DIRECTIONS)):
            @pl.when(inside(*DIRECTIONS[index]))
            def _(index=index):
                copy(l, rnd, index).wait_send()

    def put(l, rnd, x, values):
        lev = levels[l]
        edge[rnd][x + 1] = values
        for b in range(COMP):
            side_out[rnd][0, x, pl.ds(b, 1), :] = values[b * lev.yp : b * lev.yp + 1]
            side_out[rnd][1, x, pl.ds(b, 1), :] = values[b * lev.yp + lev.y - 1 : b * lev.yp + lev.y]
        return values

    def convert(l, rnd, x):
        lev = levels[l]
        for start, values in (
            (0, edge[rnd][x]),
            (lev.rows, jnp.concatenate([side[rnd][0, x], side[rnd][1, x]], axis=0)),
        ):
            a, b = split(values)
            high[l][x, pl.ds(start, values.shape[0]), :] = a
            low[l][x, pl.ds(start, values.shape[0]), :] = b

    def apply_pair(l, x0):
        lev = levels[l]
        halves = []
        for i in range(lev.wide):
            a = high[l][pl.ds(x0 + i, 3)].reshape(3 * lev.depth, 128)
            b = low[l][pl.ds(x0 + i, 3)].reshape(3 * lev.depth, 128)
            halves.append(jnp.concatenate([a, a, b], axis=0))
        rhs = halves[0] if lev.wide == 1 else jnp.concatenate(halves, axis=1)
        product = jnp.dot(weight[l][...], rhs, preferred_element_type=F32)
        lane = lax.broadcasted_iota(jnp.int32, (lev.rows, 128), 1)
        sums = []
        for i in range(lev.wide):
            below, centre, above = [
                product[k * lev.rows : (k + 1) * lev.rows, i * 128 : (i + 1) * 128] for k in range(3)
            ]
            below = jnp.where(lane == 0, 0.0, pltpu.roll(below, 1, 1))
            above = jnp.where(lane == 127, 0.0, pltpu.roll(above, 127, 1))
            sums.append(centre + below + above)
        return sums

    def sweep(l, rnd, store):
        lev = levels[l]

        def pair(p):
            x0 = p * lev.wide
            for i, summed in enumerate(apply_pair(l, x0)):
                store(x0 + i, summed)

        def convert_loop(low_x, high_x):
            lax.fori_loop(low_x, high_x, lambda x, _: (convert(l, rnd, x), 0)[1], 0)

        receive(l, rnd, FACES_Y)
        if lev.pairs > 2:
            convert_loop(1, lev.x + 1)
            lax.fori_loop(1, lev.pairs - 1, lambda p, _: (pair(p), 0)[1], 0)
            receive(l, rnd, FACES_X)
            convert(l, rnd, 0)
            convert(l, rnd, lev.x + 1)
            lax.fori_loop(0, 2, lambda p, _: (pair(p * (lev.pairs - 1)), 0)[1], 0)
        else:
            receive(l, rnd, FACES_X)
            convert_loop(0, lev.x + 2)
            lax.fori_loop(0, lev.pairs, lambda p, _: (pair(p), 0)[1], 0)

    def build_weight(l):
        lev = levels[l]
        total = 9 * lev.depth
        row = lax.broadcasted_iota(jnp.int32, (lev.yp, total), 0)
        lane = lax.broadcasted_iota(jnp.int32, (lev.rows, total), 1)
        pos = jnp.broadcast_to(place[l][...], (lev.yp, total))
        pos = jnp.where(row < lev.y, pos, -100)
        bands = [pos == row + oy for oy in (-1, 0, 1)]
        middle = jnp.logical_and(lane >= 3 * lev.depth, lane < 6 * lev.depth)
        for oz in range(3):
            blocks = []
            for a in range(COMP):
                block = jnp.zeros((lev.yp, total), F32)
                for oy in range(3):
                    at = oy * 15 + oz * COMP + a
                    block = jnp.where(bands[oy], spread[l][at : at + 1, :], block)
                blocks.append(block)
            if lev.rows > COMP * lev.yp:
                blocks.append(jnp.zeros((lev.rows - COMP * lev.yp, total), F32))
            block = jnp.concatenate(blocks, axis=0)
            upper = block.astype(BF16).astype(F32)
            weight[l][pl.ds(oz * lev.rows, lev.rows), :] = jnp.where(middle, block - upper, upper).astype(BF16)

    def relax(lev):
        pieces = [jnp.full((lev.yp, 128), diag_ref[a], F32) for a in range(COMP)]
        if lev.rows > COMP * lev.yp:
            pieces.append(jnp.zeros((lev.rows - COMP * lev.yp, 128), F32))
        return jnp.concatenate(pieces, axis=0)

    def coarse_means(l):
        fine, lev = levels[l], levels[l + 1]
        scale = relax(lev)
        for x in range(lev.x):
            if l == 0:
                c = 0.5 * (conduct_ref[:, 2 * x] + conduct_ref[:, 2 * x + 1])
                c = c.reshape(fine.rows, 128)
            else:
                c = 0.5 * (conduct[l][2 * x] + conduct[l][2 * x + 1])
            s = 0.5 * (share[l][2 * x] + share[l][2 * x + 1])
            c2 = jnp.concatenate(split(c), axis=0)
            s2 = jnp.concatenate(split(s), axis=0)
            both = jnp.dot(mean_m[l][...], jnp.concatenate([c2, s2], axis=1), preferred_element_type=F32)
            conduct[l + 1][x] = jnp.maximum(both[:, :128], 0.01)
            share[l + 1][x] = both[:, 128:]
            gain[l + 1][x] = scale * both[:, 128:]

    def restrict(l, rnd):
        fine, lev = levels[l], levels[l + 1]
        receive(l, rnd, FACES_Y + FACES_X)
        columns = []
        for x in range(lev.x):
            parts = []
            for ref in (edge[rnd], side[rnd].at[0], side[rnd].at[1]):
                parts.append(sum(WEIGHTS[t] * ref[2 * x + t] for t in range(4)))
            columns.append(jnp.concatenate(split(jnp.concatenate(parts, axis=0)), axis=0))
        rhs = columns[0] if lev.x == 1 else jnp.concatenate(columns, axis=1)
        product = jnp.dot(restrict_m[l][...], rhs, preferred_element_type=F32)
        nxt = first_round[l + 1]
        for x in range(lev.x):
            f = product[:, x * 128 : (x + 1) * 128]
            force[l + 1][x] = f
            g = f / conduct[l + 1][x]
            ratio[l + 1][x] = g
            v = gain[l + 1][x] * g
            state[l + 1][x] = v
            put(l + 1, nxt, x, share[l + 1][x] * v)
        send(l + 1, nxt)

    fine = levels[0]

    def start(x, _):
        s = mask_ref[x].astype(F32)
        s = jnp.concatenate([s] * COMP, axis=0)
        share[0][x] = s
        put(0, 0, x, s * guess_ref[:, x].reshape(fine.rows, 128))
        return 0

    lax.fori_loop(0, fine.x, start, 0)
    pl.semaphore_wait(barrier, neighbours)
    send(0, 0)

    def prepare(x, _):
        f = right_ref[:, x].reshape(fine.rows, 128)
        ratio[0][x] = f / conduct_ref[:, x].reshape(fine.rows, 128)
        gain[0][x] = relax(fine) * share[0][x]
        return 0

    lax.fori_loop(0, fine.x, prepare, 0)
    for l in range(LEVELS):
        build_weight(l)
    for l in range(LEVELS - 1):
        coarse_means(l)

    def first(x, summed):
        v = guess_ref[:, x].reshape(fine.rows, 128) + gain[0][x] * (ratio[0][x] - summed)
        state[0][x] = v
        put(0, 1, x, share[0][x] * v)

    def second(x, summed):
        v = state[0][x] + gain[0][x] * (ratio[0][x] - summed)
        outs[0][:, x] = v.reshape(COMP, fine.y, 128)
        put(0, 2, x, share[0][x] * v)

    def third(x, summed):
        f = right_ref[:, x].reshape(fine.rows, 128)
        c = conduct_ref[:, x].reshape(fine.rows, 128)
        put(0, 3, x, share[0][x] * (f - c * summed))

    for rnd, store in enumerate((first, second, third)):
        sweep(0, rnd, store)
        send(0, rnd + 1)

    for l in range(1, LEVELS):
        lev, base = levels[l], first_round[l]
        restrict(l - 1, base - 1)

        def smooth(x, summed, l=l, lev=lev, base=base):
            v = state[l][x] + gain[l][x] * (ratio[l][x] - summed)
            if l < LEVELS - 1:
                outs[l][:, x] = v[: COMP * lev.yp].reshape(COMP, lev.y, 128)
            put(l, base + 1, x, share[l][x] * v)

        def remain(x, summed, l=l, lev=lev, base=base):
            r = share[l][x] * (force[l][x] - conduct[l][x] * summed)
            if l < LEVELS - 1:
                put(l, base + 2, x, r)
            else:
                outs[l][:, x] = r[: COMP * lev.yp].reshape(COMP, lev.yp, 128)[:, : lev.y]

        sweep(l, base, smooth)
        send(l, base + 1)
        sweep(l, base + 1, remain)
        if l < LEVELS - 1:
            send(l, base + 2)

    for l in range(LEVELS):
        for rnd in range(first_round[l], first_round[l] + ROUNDS[l]):
            finish(l, rnd)


def body(count_x, count_y, initial_guess, right_side, coefficients, tunnel_mask, stencil):
    extent_x, extent_y = initial_guess.shape[1], initial_guess.shape[2]
    levels = [Level(extent_x >> l, extent_y >> l) for l in range(LEVELS)]
    diag = DAMPING / jnp.diagonal(stencil[13])
    table = stencil.reshape(3, 3, 3, COMP, COMP).transpose(1, 2, 3, 0, 4).reshape(45, 15)
    hot = np.concatenate([lev.hot for lev in levels], axis=1)
    spread_all = jnp.dot(table, hot, precision=lax.Precision.HIGHEST)
    spread, at = [], 0
    for lev in levels:
        spread.append(spread_all[:, at : at + 9 * lev.depth])
        at += 9 * lev.depth
    moves = [transfer_matrices(levels[l], levels[l + 1]) for l in range(LEVELS - 1)]
    operands = [initial_guess, right_side, coefficients, tunnel_mask, diag]
    operands += spread
    operands += [jnp.asarray(lev.pos) for lev in levels]
    operands += [jnp.asarray(m[0], BF16) for m in moves]
    operands += [jnp.asarray(m[1], BF16) for m in moves]
    vmem = pl.BlockSpec(memory_space=pltpu.VMEM)
    in_specs = [vmem] * len(operands)
    in_specs[4] = pl.BlockSpec(memory_space=pltpu.SMEM)
    scratch = [pltpu.VMEM((3 * lev.rows, 9 * lev.depth), BF16) for lev in levels]
    for _ in range(2):
        scratch += [pltpu.VMEM((lev.x + 2, lev.depth, 128), BF16) for lev in levels]
    for _ in range(6):
        scratch += [pltpu.VMEM((lev.x, lev.rows, 128), F32) for lev in levels]
    of_round = [lev for lev, n in zip(levels, ROUNDS) for _ in range(n)]
    scratch += [pltpu.VMEM((lev.x + 2, lev.rows, 128), F32) for lev in of_round]
    scratch += [pltpu.VMEM((2, lev.x + 2, 8, 128), F32) for lev in of_round]
    scratch += [pltpu.VMEM((2, lev.x, 8, 128), F32) for lev in of_round]
    scratch += [pltpu.SemaphoreType.DMA((len(of_round), len(DIRECTIONS)))] * 2
    return pl.pallas_call(
        functools.partial(kernel, levels, count_x, count_y),
        out_shape=[jax.ShapeDtypeStruct((COMP, lev.x, lev.y, 128), F32) for lev in levels],
        in_specs=in_specs,
        out_specs=[vmem] * 4,
        scratch_shapes=scratch,
        compiler_params=pltpu.CompilerParams(
            collective_id=0, has_side_effects=True, vmem_limit_bytes=48 * 1024 * 1024
        ),
    )(*operands)


def solution(mesh):
    grid = P(None, "gx", "gy", None)
    return jax.shard_map(
        functools.partial(body, mesh.shape["gx"], mesh.shape["gy"]),
        mesh=mesh,
        in_specs=(grid, grid, grid, P("gx", "gy", None), P()),
        out_specs=(grid,) * 4,
        check_vma=False,
    )
```

```python
import functools

import jax
import jax.numpy as jnp
import numpy as np
from jax import lax
from jax.experimental import pallas as pl
from jax.experimental.pallas import tpu as pltpu
from jax.sharding import PartitionSpec as P

MESH = pl.DeviceIdType.MESH
COMP = 5
DAMPING = 0.7
WEIGHTS = (0.125, 0.375, 0.375, 0.125)
LEVELS = 4
ROUNDS = (4, 3, 3, 2)
DIRECTIONS = [(dx, dy) for dx in (-1, 0, 1) for dy in (-1, 0, 1) if (dx, dy) != (0, 0)]
FAR = [(dx, dy) for dx in (-2, 2) for dy in (-1, 0, 1)]
ALL = DIRECTIONS + FAR
FACES_Y = [i for i, d in enumerate(DIRECTIONS) if d[0] == 0]
FACES_X = [i for i, d in enumerate(DIRECTIONS) if d[0] != 0]
F32, BF16 = jnp.float32, jnp.bfloat16


class Level:
    def __init__(self, extent_x, extent_y, ring, at):
        self.x, self.y, self.ring = extent_x, extent_y, ring
        self.yp = max(8, extent_y)
        self.rows = -(-COMP * self.yp // 16) * 16
        self.depth = self.rows + (32 if ring else 16)
        self.out = self.rows + (16 if ring else 0)
        self.halo = self.depth - self.rows
        pos = np.full((self.depth,), -100, np.int32)
        unknown = np.zeros((self.depth,), np.int32)
        for b in range(COMP):
            pos[b * self.yp : b * self.yp + self.y] = np.arange(self.y)
            unknown[b * self.yp : (b + 1) * self.yp] = b
            for i, y in enumerate((-1, self.y, -2, self.y + 1)[: self.halo // 8]):
                pos[self.rows + 8 * i + b], unknown[self.rows + 8 * i + b] = y, b
        self.total = 9 * self.depth
        self.at = at
        self.end = at + -(-self.total // 128) * 128
        hot = np.zeros((15, 3 * self.depth), np.float32)
        for ox in range(3):
            hot[ox * COMP + unknown, ox * self.depth + np.arange(self.depth)] = 1.0
        self.plan = np.zeros((16, self.end - at), np.float32)
        self.plan[:15, : self.total] = np.tile(hot, (1, 3))
        self.plan[15, : self.total] = np.tile(pos, 9)


def transfer_matrices(fine, coarse):
    restrict = np.zeros((coarse.rows, fine.rows + 16), np.float32)
    mean = np.zeros((coarse.rows, fine.rows), np.float32)
    for a in range(COMP):
        for j in range(coarse.y):
            row = a * coarse.yp + j
            for t in range(4):
                y = 2 * j - 1 + t
                if y < 0:
                    column = fine.rows + a
                elif y >= fine.y:
                    column = fine.rows + 8 + a
                else:
                    column = a * fine.yp + y
                restrict[row, column] = WEIGHTS[t]
            mean[row, a * fine.yp + 2 * j] = 0.5
            mean[row, a * fine.yp + 2 * j + 1] = 0.5
    return np.tile(restrict, (1, 2)), np.tile(mean, (1, 2))


def split(values):
    high = values.astype(BF16)
    return high, (values - high.astype(F32)).astype(BF16)


def kernel(levels, count_x, count_y, *refs):
    refs = list(refs)
    take = lambda n: [refs.pop(0) for _ in range(n)]
    guess_ref, right_ref, conduct_ref, mask_ref, stencil_ref, plan_ref, moves_ref = take(7)
    outs = take(4)
    weight = take(LEVELS)
    high, low = take(LEVELS), take(LEVELS)
    high2, low2 = take(LEVELS), take(LEVELS)
    conduct, share, force, ratio, gain, state = [take(LEVELS) for _ in range(6)]
    edge, side, side_out = [take(sum(ROUNDS)) for _ in range(3)]
    send_sem, recv_sem = take(2)

    at_x, at_y = lax.axis_index("gx"), lax.axis_index("gy")

    def inside(dx, dy):
        okay = None
        for shift, at, count in ((dx, at_x, count_x), (dy, at_y, count_y)):
            if shift:
                here = at >= -shift if shift < 0 else at < count - shift
                okay = here if okay is None else jnp.logical_and(okay, here)
        return okay

    first_round = [sum(ROUNDS[:l]) for l in range(LEVELS)]

    def width_of(rnd):
        return 2 if any(rnd == first_round[l] + 1 for l in range(1, LEVELS)) else 1

    def ways(l, rnd):
        return range(len(ALL) if levels[l].x == 1 and width_of(rnd) == 2 else len(DIRECTIONS))

    for l, lev in enumerate(levels):
        for rnd in range(first_round[l], first_round[l] + ROUNDS[l]):
            width = width_of(rnd)
            edge[rnd][pl.ds(0, width)] = jnp.zeros((width, lev.rows, 128), F32)
            edge[rnd][pl.ds(lev.x + width, width)] = jnp.zeros((width, lev.rows, 128), F32)
            side[rnd][...] = jnp.zeros(side[rnd].shape, F32)
            side_out[rnd][...] = jnp.zeros(side_out[rnd].shape, F32)

    barrier = pltpu.get_barrier_semaphore()
    for dx, dy in ALL:
        @pl.when(inside(dx, dy))
        def _(dx=dx, dy=dy):
            pl.semaphore_signal(barrier, inc=1, device_id=(at_x + dx, at_y + dy), device_id_type=MESH)

    def span(at, count, reach):
        total = 1
        for shift in range(1, reach + 1):
            total = total + jnp.where(at >= shift, 1, 0) + jnp.where(at < count - shift, 1, 0)
        return total

    neighbours = span(at_x, count_x, 2) * span(at_y, count_y, 1) - 1

    def copy(l, rnd, index):
        lev, width = levels[l], width_of(rnd)
        dx, dy = ALL[index]
        if lev.x >= width:
            mine, theirs, n = (lev.x - width if dx > 0 else 0), (0 if dx > 0 else lev.x + width), width
        else:
            mine, theirs, n = 0, width - dx, 1
        if dx == 0:
            mine, theirs, n = 0, width, lev.x
        if dy == 0:
            src, dst = edge[rnd].at[pl.ds(width + mine, n)], edge[rnd].at[pl.ds(theirs, n)]
        else:
            out_at, in_at = (1, 0) if dy > 0 else (0, 1)
            src = side_out[rnd].at[out_at, pl.ds(mine, n)]
            dst = side[rnd].at[in_at, pl.ds(theirs, n)]
        return pltpu.make_async_remote_copy(
            src_ref=src,
            dst_ref=dst,
            send_sem=send_sem.at[rnd, index],
            recv_sem=recv_sem.at[rnd, index],
            device_id=(at_x + dx, at_y + dy),
            device_id_type=MESH,
        )

    def send(l, rnd):
        for index in [i for i in ways(l, rnd) if i not in FACES_Y] + FACES_Y:
            @pl.when(inside(*ALL[index]))
            def _(index=index):
                copy(l, rnd, index).start()

    def receive(l, rnd, which):
        for index in which:
            dx, dy = ALL[index]
            @pl.when(inside(-dx, -dy))
            def _(index=index):
                copy(l, rnd, index).wait_recv()

    def finish(l, rnd):
        for index in ways(l, rnd):
            @pl.when(inside(*ALL[index]))
            def _(index=index):
                copy(l, rnd, index).wait_send()

    def put(l, rnd, x, values):
        lev, width = levels[l], width_of(rnd)
        edge[rnd][x + width] = values
        for b in range(COMP):
            for i in range(width):
                y = b * lev.yp + i
                side_out[rnd][0, x, pl.ds(8 * i + b, 1), :] = values[y : y + 1]
                y = b * lev.yp + lev.y - 1 - i
                side_out[rnd][1, x, pl.ds(8 * i + b, 1), :] = values[y : y + 1]

    def convert(l, rnd, x):
        lev = levels[l]
        halo = [side[rnd][i, x, pl.ds(k, 8), :] for k in range(0, lev.halo // 2, 8) for i in range(2)]
        for start, values in ((0, edge[rnd][x]), (lev.rows, jnp.concatenate(halo, axis=0))):
            a, b = split(values)
            high[l][x, pl.ds(start, values.shape[0]), :] = a
            low[l][x, pl.ds(start, values.shape[0]), :] = b

    def apply_group(l, x0, n, high_ref, low_ref):
        lev = levels[l]
        halves = []
        for i in range(n):
            a = high_ref[pl.ds(x0 + i, 3)].reshape(3 * lev.depth, 128)
            b = low_ref[pl.ds(x0 + i, 3)].reshape(3 * lev.depth, 128)
            halves.append(jnp.concatenate([a, a, b], axis=0))
        rhs = halves[0] if n == 1 else jnp.concatenate(halves, axis=1)
        product = jnp.dot(weight[l][...], rhs, preferred_element_type=F32)
        lane = lax.broadcasted_iota(jnp.int32, (lev.out, 128), 1)
        sums = []
        for i in range(n):
            below, centre, above = [
                product[k * lev.out : (k + 1) * lev.out, i * 128 : (i + 1) * 128] for k in range(3)
            ]
            below = jnp.where(lane == 0, 0.0, pltpu.roll(below, 1, 1))
            above = jnp.where(lane == 127, 0.0, pltpu.roll(above, 127, 1))
            sums.append(centre + below + above)
        return sums

    def sweep_fine(rnd, store):
        lev = levels[0]
        pairs = lev.x // 2

        def pair(p, _):
            for i, summed in enumerate(apply_group(0, 2 * p, 2, high[0], low[0])):
                store(2 * p + i, summed)
            return 0

        receive(0, rnd, FACES_Y)
        lax.fori_loop(1, lev.x + 1, lambda x, _: (convert(0, rnd, x), 0)[1], 0)
        lax.fori_loop(1, pairs - 1, pair, 0)
        receive(0, rnd, FACES_X)
        convert(0, rnd, 0)
        convert(0, rnd, lev.x + 1)
        lax.fori_loop(0, 2, lambda p, _: pair(p * (pairs - 1), 0), 0)

    def build_weight(l):
        lev = levels[l]
        total = lev.total
        segment = pl.ds(lev.at, lev.end - lev.at)
        spread = sum(
            jnp.dot(
                jnp.concatenate([stencil_ref[9 * ox + i] for i in range(9)], axis=0),
                plan_ref[pl.ds(COMP * ox, COMP), segment],
                precision=lax.Precision.HIGHEST,
                preferred_element_type=F32,
            )
            for ox in range(3)
        )[:, :total]
        place = plan_ref[pl.ds(15, 1), segment][:, :total].astype(jnp.int32)
        row = lax.broadcasted_iota(jnp.int32, (lev.yp, total), 0)
        lane = lax.broadcasted_iota(jnp.int32, (lev.out, total), 1)
        pos = jnp.where(row < lev.y, jnp.broadcast_to(place, (lev.yp, total)), -100)
        ring_pos = jnp.broadcast_to(place, (COMP, total))
        bands = [pos == row + oy for oy in (-1, 0, 1)]
        middle = jnp.logical_and(lane >= 3 * lev.depth, lane < 6 * lev.depth)
        for oz in range(3):
            blocks = []
            for a in range(COMP):
                block = jnp.zeros((lev.yp, total), F32)
                for oy in range(3):
                    at = oy * 15 + oz * COMP + a
                    block = jnp.where(bands[oy], spread[at : at + 1, :], block)
                blocks.append(block)
            if lev.rows > COMP * lev.yp:
                blocks.append(jnp.zeros((lev.rows - COMP * lev.yp, total), F32))
            if lev.ring:
                for y in (-1, lev.y):
                    block = jnp.zeros((COMP, total), F32)
                    for oy in range(3):
                        at = oy * 15 + oz * COMP
                        block = jnp.where(ring_pos == y + oy - 1, spread[at : at + COMP, :], block)
                    blocks += [block, jnp.zeros((8 - COMP, total), F32)]
            block = jnp.concatenate(blocks, axis=0)
            upper = block.astype(BF16).astype(F32)
            weight[l][pl.ds(oz * lev.out, lev.out), :] = jnp.where(middle, block - upper, upper).astype(BF16)

    def relax(lev):
        centre = stencil_ref[13]
        pieces = [
            DAMPING / jnp.broadcast_to(centre[a : a + 1, a : a + 1], (lev.yp, 128)) for a in range(COMP)
        ]
        if lev.rows > COMP * lev.yp:
            pieces.append(jnp.zeros((lev.rows - COMP * lev.yp, 128), F32))
        return jnp.concatenate(pieces, axis=0)

    def matrix(l, which):
        fine, lev = levels[l], levels[l + 1]
        at = sum(2 * levels[i + 1].rows for i in range(l)) + which * lev.rows
        return moves_ref[pl.ds(at, lev.rows), pl.ds(0, 2 * (fine.rows + (0 if which else 16)))]

    def coarse_means(l):
        fine, lev = levels[l], levels[l + 1]
        scale = relax(lev)
        for x in range(lev.x):
            if l == 0:
                c = 0.5 * (conduct_ref[:, 2 * x] + conduct_ref[:, 2 * x + 1])
                c = c.reshape(fine.rows, 128)
            else:
                c = 0.5 * (conduct[l][2 * x] + conduct[l][2 * x + 1])
            s = 0.5 * (share[l][2 * x] + share[l][2 * x + 1])
            c2 = jnp.concatenate(split(c), axis=0)
            s2 = jnp.concatenate(split(s), axis=0)
            both = jnp.dot(matrix(l, 1), jnp.concatenate([c2, s2], axis=1), preferred_element_type=F32)
            conduct[l + 1][x] = jnp.maximum(both[:, :128], 0.01)
            share[l + 1][x] = both[:, 128:]
            gain[l + 1][x] = scale * both[:, 128:]
            put(l + 1, first_round[l + 1], x, scale * both[:, 128:] * both[:, 128:])
        send(l + 1, first_round[l + 1])

    def restrict(l, rnd):
        fine, lev = levels[l], levels[l + 1]
        receive(l, rnd, FACES_Y + FACES_X)
        columns = []
        for x in range(lev.x):
            parts = []
            for ref in (edge[rnd], side[rnd].at[0], side[rnd].at[1]):
                parts.append(sum(WEIGHTS[t] * ref[2 * x + t] for t in range(4)))
            columns.append(jnp.concatenate(split(jnp.concatenate(parts, axis=0)), axis=0))
        rhs = columns[0] if lev.x == 1 else jnp.concatenate(columns, axis=1)
        product = jnp.dot(matrix(l, 0), rhs, preferred_element_type=F32)
        nxt = first_round[l + 1] + 1
        for x in range(lev.x):
            f = product[:, x * 128 : (x + 1) * 128]
            force[l + 1][x] = f
            g = f / conduct[l + 1][x]
            v = gain[l + 1][x] * g
            state[l + 1][x] = v
            put(l + 1, nxt, x, share[l + 1][x] * v)
        send(l + 1, nxt)

    fine = levels[0]

    def start(x, _):
        s = mask_ref[x].astype(F32)
        s = jnp.concatenate([s] * COMP, axis=0)
        share[0][x] = s
        put(0, 0, x, s * guess_ref[:, x].reshape(fine.rows, 128))
        return 0

    lax.fori_loop(0, fine.x, start, 0)
    pl.semaphore_wait(barrier, neighbours)
    send(0, 0)

    scale = relax(fine)

    def prepare(x, _):
        f = right_ref[:, x].reshape(fine.rows, 128)
        ratio[0][x] = f / conduct_ref[:, x].reshape(fine.rows, 128)
        gain[0][x] = scale * share[0][x]
        return 0

    lax.fori_loop(0, fine.x, prepare, 0)
    for l in range(LEVELS - 1):
        coarse_means(l)
    for l in range(LEVELS):
        build_weight(l)
    for l in range(1, LEVELS):
        for ref in (high2[l], low2[l]):
            ref[:, pl.ds(levels[l].out, 16), :] = jnp.zeros((levels[l].x + 2, 16, 128), BF16)

    def first(x, summed):
        v = guess_ref[:, x].reshape(fine.rows, 128) + gain[0][x] * (ratio[0][x] - summed)
        state[0][x] = v
        put(0, 1, x, share[0][x] * v)

    def second(x, summed):
        v = state[0][x] + gain[0][x] * (ratio[0][x] - summed)
        outs[0][:, x] = v.reshape(COMP, fine.y, 128)
        put(0, 2, x, share[0][x] * v)

    def third(x, summed):
        f = right_ref[:, x].reshape(fine.rows, 128)
        c = conduct_ref[:, x].reshape(fine.rows, 128)
        put(0, 3, x, share[0][x] * (f - c * summed))

    for rnd, store in enumerate((first, second, third)):
        sweep_fine(rnd, store)
        send(0, rnd + 1)

    for l in range(1, LEVELS):
        lev, base = levels[l], first_round[l]
        restrict(l - 1, base - 1)

        wide = 2 if lev.x > 1 else 3
        receive(l, base + 1, ways(l, base + 1))
        lax.fori_loop(0, lev.x + 4, lambda x, _, l=l, base=base: (convert(l, base + 1, x), 0)[1], 0)
        receive(l, base, FACES_Y + FACES_X)

        def smooth(p, _, l=l, lev=lev, base=base, wide=wide):
            for i, summed in enumerate(apply_group(l, p * wide, wide, high[l], low[l])):
                x = p * wide + i
                m = [edge[base + 1][x + 1]] + [side[base + 1][k, x + 1, pl.ds(0, 8), :] for k in range(2)]
                q = [edge[base][x], side[base][0, x], side[base][1, x]]
                m = 2.0 * jnp.concatenate(m, axis=0) - jnp.concatenate(q, axis=0) * summed
                a, b = split(m)
                high2[l][x, pl.ds(0, lev.out), :] = a
                low2[l][x, pl.ds(0, lev.out), :] = b
                if l < LEVELS - 1:
                    @pl.when(jnp.logical_and(x >= 1, x <= lev.x))
                    def _(summed=summed, x=x):
                        v = 2.0 * state[l][x - 1] - gain[l][x - 1] * summed[: lev.rows]
                        outs[l][:, x - 1] = v[: COMP * lev.yp].reshape(COMP, lev.y, 128)
            return 0

        def remain(p, _, l=l, lev=lev, base=base):
            n = min(2, lev.x)
            for i, summed in enumerate(apply_group(l, p * n, n, high2[l], low2[l])):
                x = p * n + i
                r = share[l][x] * (force[l][x] - conduct[l][x] * summed[: lev.rows])
                if l < LEVELS - 1:
                    put(l, base + 2, x, r)
                else:
                    outs[l][:, x] = r[: COMP * lev.yp].reshape(COMP, lev.yp, 128)[:, : lev.y]
            return 0

        lax.fori_loop(0, (lev.x + 2) // wide, smooth, 0)
        lax.fori_loop(0, max(1, lev.x // 2), remain, 0)
        if l < LEVELS - 1:
            send(l, base + 2)

    for l in range(LEVELS):
        for rnd in range(first_round[l], first_round[l] + ROUNDS[l]):
            finish(l, rnd)


def body(count_x, count_y, initial_guess, right_side, coefficients, tunnel_mask, stencil):
    extent_x, extent_y = initial_guess.shape[1], initial_guess.shape[2]
    levels, at = [], 0
    for l in range(LEVELS):
        levels.append(Level(extent_x >> l, extent_y >> l, l > 0, at))
        at = levels[-1].end
    plan = np.concatenate([lev.plan for lev in levels], axis=1)
    moves = [m for l in range(LEVELS - 1) for m in transfer_matrices(levels[l], levels[l + 1])]
    widest = -(-max(m.shape[1] for m in moves) // 128) * 128
    moves = np.concatenate([np.pad(m, ((0, 0), (0, widest - m.shape[1]))) for m in moves], axis=0)
    operands = [initial_guess, right_side, coefficients, tunnel_mask, stencil]
    operands += [jnp.asarray(plan), jnp.asarray(moves, BF16)]
    vmem = pl.BlockSpec(memory_space=pltpu.VMEM)
    scratch = [pltpu.VMEM((3 * lev.out, lev.total), BF16) for lev in levels]
    for extra in (4, 4, 2, 2):
        scratch += [pltpu.VMEM((lev.x + extra, lev.depth, 128), BF16) for lev in levels]
    for _ in range(6):
        scratch += [pltpu.VMEM((lev.x, lev.rows, 128), F32) for lev in levels]
    of_round = [(lev, 2 if lev.ring and i == 1 else 1) for lev, n in zip(levels, ROUNDS) for i in range(n)]
    scratch += [pltpu.VMEM((lev.x + 2 * width, lev.rows, 128), F32) for lev, width in of_round]
    scratch += [pltpu.VMEM((2, lev.x + 2 * width, 8 * width, 128), F32) for lev, width in of_round]
    scratch += [pltpu.VMEM((2, lev.x, 8 * width, 128), F32) for lev, width in of_round]
    scratch += [pltpu.SemaphoreType.DMA((len(of_round), len(ALL)))] * 2
    return pl.pallas_call(
        functools.partial(kernel, levels, count_x, count_y),
        out_shape=[jax.ShapeDtypeStruct((COMP, lev.x, lev.y, 128), F32) for lev in levels],
        in_specs=[vmem] * len(operands),
        out_specs=[vmem] * 4,
        scratch_shapes=scratch,
        compiler_params=pltpu.CompilerParams(
            collective_id=0, has_side_effects=True, vmem_limit_bytes=48 * 1024 * 1024
        ),
    )(*operands)


def solution(mesh):
    grid = P(None, "gx", "gy", None)
    return jax.shard_map(
        functools.partial(body, mesh.shape["gx"], mesh.shape["gy"]),
        mesh=mesh,
        in_specs=(grid, grid, grid, P("gx", "gy", None), P()),
        out_specs=(grid,) * 4,
        check_vma=False,
    )
```

```python
import functools

import jax
import jax.numpy as jnp
import numpy as np
from jax import lax
from jax.experimental import pallas as pl
from jax.experimental.pallas import tpu as pltpu
from jax.sharding import PartitionSpec as P

MESH = pl.DeviceIdType.MESH
COMP = 5
DAMPING = 0.7
WEIGHTS = (0.125, 0.375, 0.375, 0.125)
LEVELS = 4
ROUNDS = (4, 3, 3, 2)
DIRECTIONS = [(dx, dy) for dx in (-1, 0, 1) for dy in (-1, 0, 1) if (dx, dy) != (0, 0)]
FAR = [(dx, dy) for dx in (-2, 2) for dy in (-1, 0, 1)]
ALL = DIRECTIONS + FAR
FACES_Y = [i for i, d in enumerate(DIRECTIONS) if d[0] == 0]
FACES_X = [i for i, d in enumerate(DIRECTIONS) if d[0] != 0]
F32, BF16 = jnp.float32, jnp.bfloat16


class Level:
    def __init__(self, extent_x, extent_y, ring, at):
        self.x, self.y, self.ring = extent_x, extent_y, ring
        self.yp = max(8, extent_y)
        self.rows = -(-COMP * self.yp // 16) * 16
        self.depth = self.rows + (32 if ring else 16)
        self.out = self.rows + (16 if ring else 0)
        self.halo = self.depth - self.rows
        pos = np.full((self.depth,), -100, np.int32)
        unknown = np.zeros((self.depth,), np.int32)
        for b in range(COMP):
            pos[b * self.yp : b * self.yp + self.y] = np.arange(self.y)
            unknown[b * self.yp : (b + 1) * self.yp] = b
            for i, y in enumerate((-1, self.y, -2, self.y + 1)[: self.halo // 8]):
                pos[self.rows + 8 * i + b], unknown[self.rows + 8 * i + b] = y, b
        self.total = 9 * self.depth
        self.at = at
        self.end = at + -(-self.total // 128) * 128
        hot = np.zeros((15, 3 * self.depth), np.float32)
        for ox in range(3):
            hot[ox * COMP + unknown, ox * self.depth + np.arange(self.depth)] = 1.0
        self.plan = np.zeros((16, self.end - at), np.float32)
        self.plan[:15, : self.total] = np.tile(hot, (1, 3))
        self.plan[15, : self.total] = np.tile(pos, 9)


def transfer_matrices(fine, coarse):
    restrict = np.zeros((coarse.rows, fine.rows + 16), np.float32)
    mean = np.zeros((coarse.rows, fine.rows), np.float32)
    for a in range(COMP):
        for j in range(coarse.y):
            row = a * coarse.yp + j
            for t in range(4):
                y = 2 * j - 1 + t
                if y < 0:
                    column = fine.rows + a
                elif y >= fine.y:
                    column = fine.rows + 8 + a
                else:
                    column = a * fine.yp + y
                restrict[row, column] = WEIGHTS[t]
            mean[row, a * fine.yp + 2 * j] = 0.5
            mean[row, a * fine.yp + 2 * j + 1] = 0.5
    return np.tile(restrict, (1, 2)), np.tile(mean, (1, 2))


def split(values):
    high = values.astype(BF16)
    return high, (values - high.astype(F32)).astype(BF16)


def kernel(levels, count_x, count_y, *refs):
    refs = list(refs)
    take = lambda n: [refs.pop(0) for _ in range(n)]
    stencil_ref = refs.pop(0)
    sources, targets = take(6), take(4)
    loaded = guess_ref, mask_ref, right_ref, conduct_ref, plan_ref, moves_ref = take(6)
    outs = take(4)
    weight = take(LEVELS)
    high, low = take(LEVELS), take(LEVELS)
    high2, low2 = take(LEVELS), take(LEVELS)
    conduct, share, force, ratio, gain, state = [take(LEVELS) for _ in range(6)]
    edge, side, side_out = [take(sum(ROUNDS)) for _ in range(3)]
    send_sem, recv_sem, load_sem, store_sem = take(4)
    loads = [pltpu.make_async_copy(a, b, load_sem.at[i]) for i, (a, b) in enumerate(zip(sources, loaded))]
    stores = [pltpu.make_async_copy(a, b, store_sem.at[i]) for i, (a, b) in enumerate(zip(outs, targets))]
    for load in loads:
        load.start()

    at_x, at_y = lax.axis_index("gx"), lax.axis_index("gy")

    def inside(dx, dy):
        okay = None
        for shift, at, count in ((dx, at_x, count_x), (dy, at_y, count_y)):
            if shift:
                here = at >= -shift if shift < 0 else at < count - shift
                okay = here if okay is None else jnp.logical_and(okay, here)
        return okay

    first_round = [sum(ROUNDS[:l]) for l in range(LEVELS)]

    def width_of(rnd):
        return 2 if any(rnd == first_round[l] + 1 for l in range(1, LEVELS)) else 1

    def ways(l, rnd):
        return range(len(ALL) if levels[l].x == 1 and width_of(rnd) == 2 else len(DIRECTIONS))

    for l, lev in enumerate(levels):
        for rnd in range(first_round[l], first_round[l] + ROUNDS[l]):
            width = width_of(rnd)
            edge[rnd][pl.ds(0, width)] = jnp.zeros((width, lev.rows, 128), F32)
            edge[rnd][pl.ds(lev.x + width, width)] = jnp.zeros((width, lev.rows, 128), F32)
            side[rnd][...] = jnp.zeros(side[rnd].shape, F32)
            side_out[rnd][...] = jnp.zeros(side_out[rnd].shape, F32)

    barrier = pltpu.get_barrier_semaphore()
    for dx, dy in ALL:
        @pl.when(inside(dx, dy))
        def _(dx=dx, dy=dy):
            pl.semaphore_signal(barrier, inc=1, device_id=(at_x + dx, at_y + dy), device_id_type=MESH)

    def span(at, count, reach):
        total = 1
        for shift in range(1, reach + 1):
            total = total + jnp.where(at >= shift, 1, 0) + jnp.where(at < count - shift, 1, 0)
        return total

    neighbours = span(at_x, count_x, 2) * span(at_y, count_y, 1) - 1

    def copy(l, rnd, index):
        lev, width = levels[l], width_of(rnd)
        dx, dy = ALL[index]
        if lev.x >= width:
            mine, theirs, n = (lev.x - width if dx > 0 else 0), (0 if dx > 0 else lev.x + width), width
        else:
            mine, theirs, n = 0, width - dx, 1
        if dx == 0:
            mine, theirs, n = 0, width, lev.x
        if dy == 0:
            src, dst = edge[rnd].at[pl.ds(width + mine, n)], edge[rnd].at[pl.ds(theirs, n)]
        else:
            out_at, in_at = (1, 0) if dy > 0 else (0, 1)
            src = side_out[rnd].at[out_at, pl.ds(mine, n)]
            dst = side[rnd].at[in_at, pl.ds(theirs, n)]
        return pltpu.make_async_remote_copy(
            src_ref=src,
            dst_ref=dst,
            send_sem=send_sem.at[rnd, index],
            recv_sem=recv_sem.at[rnd, index],
            device_id=(at_x + dx, at_y + dy),
            device_id_type=MESH,
        )

    def send(l, rnd):
        for index in [i for i in ways(l, rnd) if i not in FACES_Y] + FACES_Y:
            @pl.when(inside(*ALL[index]))
            def _(index=index):
                copy(l, rnd, index).start()

    def receive(l, rnd, which):
        for index in which:
            dx, dy = ALL[index]
            @pl.when(inside(-dx, -dy))
            def _(index=index):
                copy(l, rnd, index).wait_recv()

    def finish(l, rnd):
        for index in ways(l, rnd):
            @pl.when(inside(*ALL[index]))
            def _(index=index):
                copy(l, rnd, index).wait_send()

    def put(l, rnd, x, values):
        lev, width = levels[l], width_of(rnd)
        edge[rnd][x + width] = values
        for b in range(COMP):
            for i in range(width):
                y = b * lev.yp + i
                side_out[rnd][0, x, pl.ds(8 * i + b, 1), :] = values[y : y + 1]
                y = b * lev.yp + lev.y - 1 - i
                side_out[rnd][1, x, pl.ds(8 * i + b, 1), :] = values[y : y + 1]

    def convert_rows(l, x, first_row, values):
        a, b = split(values)
        high[l][x, pl.ds(first_row, values.shape[0]), :] = a
        low[l][x, pl.ds(first_row, values.shape[0]), :] = b

    def convert_plane(l, rnd, x):
        convert_rows(l, x, 0, edge[rnd][x])

    def convert_halo(l, rnd, x):
        lev = levels[l]
        halo = [side[rnd][i, x, pl.ds(k, 8), :] for k in range(0, lev.halo // 2, 8) for i in range(2)]
        convert_rows(l, x, lev.rows, jnp.concatenate(halo, axis=0))

    def convert_own(l, rnd):
        start = width_of(rnd)
        loop(start, start + levels[l].x, lambda x: convert_plane(l, rnd, x))

    def loop(start, stop, step):
        lax.fori_loop(start, stop, lambda i, _: (step(i), 0)[1], 0)

    def apply_group(l, x0, n, high_ref, low_ref):
        lev = levels[l]
        halves = []
        for i in range(n):
            a = high_ref[pl.ds(x0 + i, 3)].reshape(3 * lev.depth, 128)
            b = low_ref[pl.ds(x0 + i, 3)].reshape(3 * lev.depth, 128)
            halves.append(jnp.concatenate([a, a, b], axis=0))
        rhs = halves[0] if n == 1 else jnp.concatenate(halves, axis=1)
        product = jnp.dot(weight[l][...], rhs, preferred_element_type=F32)
        lane = lax.broadcasted_iota(jnp.int32, (lev.out, 128), 1)
        sums = []
        for i in range(n):
            below, centre, above = [
                product[k * lev.out : (k + 1) * lev.out, i * 128 : (i + 1) * 128] for k in range(3)
            ]
            below = jnp.where(lane == 0, 0.0, pltpu.roll(below, 1, 1))
            above = jnp.where(lane == 127, 0.0, pltpu.roll(above, 127, 1))
            sums.append(centre + below + above)
        return sums

    def sweep_fine(rnd, store):
        lev = levels[0]
        pairs = lev.x // 2

        def pair(p, _):
            for i, summed in enumerate(apply_group(0, 2 * p, 2, high[0], low[0])):
                store(2 * p + i, summed)
            return 0

        convert_own(0, rnd)
        receive(0, rnd, FACES_Y)
        loop(1, lev.x + 1, lambda x: convert_halo(0, rnd, x))
        lax.fori_loop(1, pairs - 1, pair, 0)
        receive(0, rnd, FACES_X)
        for x in (0, lev.x + 1):
            convert_plane(0, rnd, x)
            convert_halo(0, rnd, x)
        lax.fori_loop(0, 2, lambda p, _: pair(p * (pairs - 1), 0), 0)

    def build_weight(l):
        lev = levels[l]
        total = lev.total
        segment = pl.ds(lev.at, lev.end - lev.at)
        spread = sum(
            jnp.dot(
                jnp.concatenate([stencil_ref[9 * ox + i] for i in range(9)], axis=0),
                plan_ref[pl.ds(COMP * ox, COMP), segment],
                precision=lax.Precision.HIGHEST,
                preferred_element_type=F32,
            )
            for ox in range(3)
        )[:, :total]
        place = plan_ref[pl.ds(15, 1), segment][:, :total].astype(jnp.int32)
        row = lax.broadcasted_iota(jnp.int32, (lev.yp, total), 0)
        lane = lax.broadcasted_iota(jnp.int32, (lev.out, total), 1)
        pos = jnp.where(row < lev.y, jnp.broadcast_to(place, (lev.yp, total)), -100)
        ring_pos = jnp.broadcast_to(place, (COMP, total))
        bands = [pos == row + oy for oy in (-1, 0, 1)]
        middle = jnp.logical_and(lane >= 3 * lev.depth, lane < 6 * lev.depth)
        for oz in range(3):
            blocks = []
            for a in range(COMP):
                block = jnp.zeros((lev.yp, total), F32)
                for oy in range(3):
                    at = oy * 15 + oz * COMP + a
                    block = jnp.where(bands[oy], spread[at : at + 1, :], block)
                blocks.append(block)
            if lev.rows > COMP * lev.yp:
                blocks.append(jnp.zeros((lev.rows - COMP * lev.yp, total), F32))
            if lev.ring:
                for y in (-1, lev.y):
                    block = jnp.zeros((COMP, total), F32)
                    for oy in range(3):
                        at = oy * 15 + oz * COMP
                        block = jnp.where(ring_pos == y + oy - 1, spread[at : at + COMP, :], block)
                    blocks += [block, jnp.zeros((8 - COMP, total), F32)]
            block = jnp.concatenate(blocks, axis=0)
            upper = block.astype(BF16).astype(F32)
            weight[l][pl.ds(oz * lev.out, lev.out), :] = jnp.where(middle, block - upper, upper).astype(BF16)

    def relax(lev):
        centre = stencil_ref[13]
        pieces = [
            DAMPING / jnp.broadcast_to(centre[a : a + 1, a : a + 1], (lev.yp, 128)) for a in range(COMP)
        ]
        if lev.rows > COMP * lev.yp:
            pieces.append(jnp.zeros((lev.rows - COMP * lev.yp, 128), F32))
        return jnp.concatenate(pieces, axis=0)

    def matrix(l, which):
        fine, lev = levels[l], levels[l + 1]
        at = sum(2 * levels[i + 1].rows for i in range(l)) + which * lev.rows
        return moves_ref[pl.ds(at, lev.rows), pl.ds(0, 2 * (fine.rows + (0 if which else 16)))]

    def coarse_means(l):
        fine, lev = levels[l], levels[l + 1]
        scale = relax(lev)
        for x in range(lev.x):
            if l == 0:
                c = 0.5 * (conduct_ref[:, 2 * x] + conduct_ref[:, 2 * x + 1])
                c = c.reshape(fine.rows, 128)
            else:
                c = 0.5 * (conduct[l][2 * x] + conduct[l][2 * x + 1])
            s = 0.5 * (share[l][2 * x] + share[l][2 * x + 1])
            c2 = jnp.concatenate(split(c), axis=0)
            s2 = jnp.concatenate(split(s), axis=0)
            both = jnp.dot(matrix(l, 1), jnp.concatenate([c2, s2], axis=1), preferred_element_type=F32)
            conduct[l + 1][x] = jnp.maximum(both[:, :128], 0.01)
            share[l + 1][x] = both[:, 128:]
            gain[l + 1][x] = scale * both[:, 128:]
            put(l + 1, first_round[l + 1], x, scale * both[:, 128:] * both[:, 128:])
        send(l + 1, first_round[l + 1])

    def restrict(l, rnd):
        fine, lev = levels[l], levels[l + 1]
        receive(l, rnd, FACES_Y + FACES_X)
        columns = []
        for x in range(lev.x):
            parts = []
            for ref in (edge[rnd], side[rnd].at[0], side[rnd].at[1]):
                parts.append(sum(WEIGHTS[t] * ref[2 * x + t] for t in range(4)))
            columns.append(jnp.concatenate(split(jnp.concatenate(parts, axis=0)), axis=0))
        rhs = columns[0] if lev.x == 1 else jnp.concatenate(columns, axis=1)
        product = jnp.dot(matrix(l, 0), rhs, preferred_element_type=F32)
        nxt = first_round[l + 1] + 1
        for x in range(lev.x):
            f = product[:, x * 128 : (x + 1) * 128]
            force[l + 1][x] = f
            g = f / conduct[l + 1][x]
            v = gain[l + 1][x] * g
            state[l + 1][x] = v
            put(l + 1, nxt, x, share[l + 1][x] * v)
        send(l + 1, nxt)

    fine = levels[0]

    def start(x, _):
        s = mask_ref[x].astype(F32)
        s = jnp.concatenate([s] * COMP, axis=0)
        share[0][x] = s
        put(0, 0, x, s * guess_ref[:, x].reshape(fine.rows, 128))
        return 0

    loads[0].wait()
    loads[1].wait()
    lax.fori_loop(0, fine.x, start, 0)
    pl.semaphore_wait(barrier, neighbours)
    send(0, 0)

    scale = relax(fine)
    for load in loads[2:]:
        load.wait()

    def prepare(x, _):
        f = right_ref[:, x].reshape(fine.rows, 128)
        ratio[0][x] = f / conduct_ref[:, x].reshape(fine.rows, 128)
        gain[0][x] = scale * share[0][x]
        return 0

    lax.fori_loop(0, fine.x, prepare, 0)
    build_weight(0)
    for l in range(1, LEVELS):
        for ref in (high2[l], low2[l]):
            ref[:, pl.ds(levels[l].out, 16), :] = jnp.zeros((levels[l].x + 2, 16, 128), BF16)

    def first(x, summed):
        v = guess_ref[:, x].reshape(fine.rows, 128) + gain[0][x] * (ratio[0][x] - summed)
        state[0][x] = v
        put(0, 1, x, share[0][x] * v)

    def second(x, summed):
        v = state[0][x] + gain[0][x] * (ratio[0][x] - summed)
        outs[0][:, x] = v.reshape(COMP, fine.y, 128)
        put(0, 2, x, share[0][x] * v)

    def third(x, summed):
        f = right_ref[:, x].reshape(fine.rows, 128)
        c = conduct_ref[:, x].reshape(fine.rows, 128)
        put(0, 3, x, share[0][x] * (f - c * summed))

    for rnd, store in enumerate((first, second, third)):
        sweep_fine(rnd, store)
        send(0, rnd + 1)
        if rnd == 0:
            for l in range(LEVELS - 1):
                coarse_means(l)
        else:
            build_weight(rnd)
        if rnd == 1:
            stores[0].start()

    for l in range(1, LEVELS):
        lev, base = levels[l], first_round[l]
        restrict(l - 1, base - 1)
        if l == 1:
            build_weight(LEVELS - 1)

        wide = 2 if lev.x > 1 else 3
        convert_own(l, base + 1)
        receive(l, base + 1, ways(l, base + 1))
        for x in (0, 1, lev.x + 2, lev.x + 3):
            convert_plane(l, base + 1, x)
        loop(0, lev.x + 4, lambda x, l=l, base=base: convert_halo(l, base + 1, x))
        receive(l, base, FACES_Y + FACES_X)

        def smooth(p, _, l=l, lev=lev, base=base, wide=wide):
            for i, summed in enumerate(apply_group(l, p * wide, wide, high[l], low[l])):
                x = p * wide + i
                m = [edge[base + 1][x + 1]] + [side[base + 1][k, x + 1, pl.ds(0, 8), :] for k in range(2)]
                q = [edge[base][x], side[base][0, x], side[base][1, x]]
                m = 2.0 * jnp.concatenate(m, axis=0) - jnp.concatenate(q, axis=0) * summed
                a, b = split(m)
                high2[l][x, pl.ds(0, lev.out), :] = a
                low2[l][x, pl.ds(0, lev.out), :] = b
                if l < LEVELS - 1:
                    @pl.when(jnp.logical_and(x >= 1, x <= lev.x))
                    def _(summed=summed, x=x):
                        v = 2.0 * state[l][x - 1] - gain[l][x - 1] * summed[: lev.rows]
                        outs[l][:, x - 1] = v[: COMP * lev.yp].reshape(COMP, lev.y, 128)
            return 0

        def remain(p, _, l=l, lev=lev, base=base):
            n = min(2, lev.x)
            for i, summed in enumerate(apply_group(l, p * n, n, high2[l], low2[l])):
                x = p * n + i
                r = share[l][x] * (force[l][x] - conduct[l][x] * summed[: lev.rows])
                if l < LEVELS - 1:
                    put(l, base + 2, x, r)
                else:
                    outs[l][:, x] = r[: COMP * lev.yp].reshape(COMP, lev.yp, 128)[:, : lev.y]
            return 0

        lax.fori_loop(0, (lev.x + 2) // wide, smooth, 0)
        if l < LEVELS - 1:
            stores[l].start()
        lax.fori_loop(0, max(1, lev.x // 2), remain, 0)
        if l < LEVELS - 1:
            send(l, base + 2)

    for l in range(LEVELS):
        for rnd in range(first_round[l], first_round[l] + ROUNDS[l]):
            finish(l, rnd)
    stores[LEVELS - 1].start()
    for store in stores:
        store.wait()


def body(count_x, count_y, initial_guess, right_side, coefficients, tunnel_mask, stencil):
    extent_x, extent_y = initial_guess.shape[1], initial_guess.shape[2]
    levels, at = [], 0
    for l in range(LEVELS):
        levels.append(Level(extent_x >> l, extent_y >> l, l > 0, at))
        at = levels[-1].end
    plan = np.concatenate([lev.plan for lev in levels], axis=1)
    moves = [m for l in range(LEVELS - 1) for m in transfer_matrices(levels[l], levels[l + 1])]
    widest = -(-max(m.shape[1] for m in moves) // 128) * 128
    moves = np.concatenate([np.pad(m, ((0, 0), (0, widest - m.shape[1]))) for m in moves], axis=0)
    operands = [stencil, initial_guess, tunnel_mask, right_side, coefficients]
    operands += [jnp.asarray(plan), jnp.asarray(moves, BF16)]
    anywhere = pl.BlockSpec(memory_space=pl.ANY)
    results = [jax.ShapeDtypeStruct((COMP, lev.x, lev.y, 128), F32) for lev in levels]
    scratch = [pltpu.VMEM(held.shape, held.dtype) for held in operands[1:] + results]
    scratch += [pltpu.VMEM((3 * lev.out, lev.total), BF16) for lev in levels]
    for extra in (4, 4, 2, 2):
        scratch += [pltpu.VMEM((lev.x + extra, lev.depth, 128), BF16) for lev in levels]
    for _ in range(6):
        scratch += [pltpu.VMEM((lev.x, lev.rows, 128), F32) for lev in levels]
    of_round = [(lev, 2 if lev.ring and i == 1 else 1) for lev, n in zip(levels, ROUNDS) for i in range(n)]
    scratch += [pltpu.VMEM((lev.x + 2 * width, lev.rows, 128), F32) for lev, width in of_round]
    scratch += [pltpu.VMEM((2, lev.x + 2 * width, 8 * width, 128), F32) for lev, width in of_round]
    scratch += [pltpu.VMEM((2, lev.x, 8 * width, 128), F32) for lev, width in of_round]
    scratch += [pltpu.SemaphoreType.DMA((len(of_round), len(ALL)))] * 2
    scratch += [pltpu.SemaphoreType.DMA((6,)), pltpu.SemaphoreType.DMA((4,))]
    return pl.pallas_call(
        functools.partial(kernel, levels, count_x, count_y),
        out_shape=results,
        in_specs=[pl.BlockSpec(memory_space=pltpu.VMEM)] + [anywhere] * 6,
        out_specs=[anywhere] * 4,
        scratch_shapes=scratch,
        compiler_params=pltpu.CompilerParams(
            collective_id=0, has_side_effects=True, vmem_limit_bytes=60 * 1024 * 1024
        ),
    )(*operands)


def solution(mesh):
    grid = P(None, "gx", "gy", None)
    return jax.shard_map(
        functools.partial(body, mesh.shape["gx"], mesh.shape["gy"]),
        mesh=mesh,
        in_specs=(grid, grid, grid, P("gx", "gy", None), P()),
        out_specs=(grid,) * 4,
        check_vma=False,
    )
```
